128 devices in a mesh: seq: 32 (over x, z_hi, y), head: 4 (over z_lo, core).
Axes of the slice: x: 4, y: 4, z: 4 (z_hi: 2, z_lo: 2; z = z_hi * 2 + z_lo), core: 2. Of those that a mesh axis runs over, the one named last changes fastest.
Arguments:
- fine_tokens: bfloat16 [10240, 3072], P('seq'), may hold values from -21 to 21
- coarse_tokens: bfloat16 [1024, 3072], P('seq'), may hold values from -21 to 21
- w_query: bfloat16 [3072, 3072], P(None, 'head'), may hold values from -0.109375 to 0.109375
- w_key: bfloat16 [3072, 3072], P(None, 'head'), may hold values from -0.109375 to 0.109375
- w_value: bfloat16 [3072, 3072], P(None, 'head'), may hold values from -0.109375 to 0.109375
- w_out: bfloat16 [3072, 3072], P('head'), may hold values from -0.109375 to 0.109375
Outputs:
- fine_out: bfloat16 [10240, 3072], P('seq', 'head')
- coarse_out: bfloat16 [1024, 3072], P('seq', 'head')
The draws below stay inside these ranges and needn't reach their ends.
All inputs are finite; a program needn't handle non-finite values.
Results may differ from the reference program's by a relative error of at most 0.017.
The reference program's roundings to bfloat16 on the way count: a program that leaves them out, or rounds other values in their place, can miss the bound.
Values may be sent and summed in bfloat16 or wider, within the bound.
No kernel may reach another device: no remote copies, remote signals or barrier semaphores. Data moves between devices by JAX's collectives and lax.ppermute only.
A program may use at most 192 MiB of HBM per device.

```python
import jax
import jax.numpy as jnp
from jax import lax

D = 3072
HEADS = 24
HEAD_DIM = 128
FINE = 10240
COARSE = 1024


def token_rows(key, row_count):
    base = jax.random.normal(key, (row_count, D), jnp.float32)
    return jnp.clip(base, -6.0, 6.0).astype(jnp.bfloat16)


def draw_fine_tokens(key, part):
    key = jax.random.fold_in(key, 11)
    return token_rows(key, FINE)


def draw_coarse_tokens(key, part):
    key = jax.random.fold_in(key, 12)
    return token_rows(key, COARSE)


def levels(key, extent, cuts, least, largest):
    loudness = 1.0
    for dim, shards_of in cuts:
        draws = jax.random.uniform(jax.random.fold_in(jax.random.fold_in(key, 6), dim), (shards_of,), jnp.float32, least / len(cuts), largest / len(cuts))
        loudness = loudness * jnp.repeat(jnp.exp(draws), extent[dim] // shards_of).reshape((-1,) + (1,) * (len(extent) - 1 - dim))
    return loudness


def noise(rng, shape, width, limit, cuts=(), held_as=jnp.bfloat16):
    array = jax.random.normal(rng, shape, jnp.float32) * width
    if len(cuts) > 0:
        array = levels(rng, shape, cuts, -0.22, 0.18) * array
    return jnp.clip(array, min=-limit, max=limit).astype(held_as)


def setup_inputs(seed: int = 0) -> dict:
    key_of = jax.random.split(jax.random.key(seed), 7)
    return {
        "fine_tokens": draw_fine_tokens(jax.random.fold_in(key_of[6], 71), 0),
        "coarse_tokens": draw_coarse_tokens(jax.random.fold_in(key_of[6], 71), 0),
        "w_query": noise(key_of[2], (D, D), D ** -0.5, 0.109375, ((1, 4),)),
        "w_key": noise(key_of[3], (D, D), D ** -0.5, 0.109375, ((1, 4),)),
        "w_value": noise(key_of[4], (D, D), D ** -0.5, 0.109375, ((1, 4),)),
        "w_out": noise(key_of[5], (D, D), D ** -0.5, 0.109375, ((0, 4),)),
    }


def one_head(operands):
    head_queries, head_keys, head_values = operands
    scores = jnp.dot(head_queries, head_keys.T, preferred_element_type=jnp.float32) * (HEAD_DIM ** -0.5)
    top_score = jnp.max(scores, axis=1, keepdims=True)
    weights = jnp.exp(scores - top_score)
    denom_sum = jnp.sum(weights, axis=1, keepdims=True)
    mixed = jnp.dot(weights.astype(jnp.bfloat16), head_values, preferred_element_type=jnp.float32)
    return (mixed / denom_sum).astype(jnp.bfloat16)


def by_heads(matrix):
    return matrix.reshape(matrix.shape[0], HEADS, HEAD_DIM).transpose(1, 0, 2)


def reference(fine_tokens, coarse_tokens, w_query, w_key, w_value, w_out):
    all_rows = jnp.concatenate([fine_tokens, coarse_tokens], axis=0)
    queries = jnp.dot(all_rows, w_query, preferred_element_type=jnp.float32).astype(jnp.bfloat16)
    key_rows = jnp.dot(all_rows, w_key, preferred_element_type=jnp.float32).astype(jnp.bfloat16)
    value_rows = jnp.dot(all_rows, w_value, preferred_element_type=jnp.float32).astype(jnp.bfloat16)
    attended = lax.map(one_head, (by_heads(queries), by_heads(key_rows), by_heads(value_rows)))
    attended = attended.transpose(1, 0, 2).reshape(all_rows.shape[0], D)
    projected = jnp.dot(attended, w_out, preferred_element_type=jnp.float32).astype(jnp.bfloat16)
    return projected[:FINE], projected[FINE:]
```

```python
import functools
import math

import jax
import jax.numpy as jnp
from jax import lax
from jax.experimental import pallas as pl
from jax.experimental.pallas import tpu as pltpu
from jax.sharding import PartitionSpec as P

BF, F32 = jnp.bfloat16, jnp.float32
D = 3072
HD = 128
FINE_ROWS, ROWS = 320, 352
HALF = ROWS // 2
COLS = 768
NX, NZH, NY, NZL, NC = 4, 2, 4, 2, 2
SCALE = math.log2(math.e) / math.sqrt(HD)
LOW, HIGH = 2.0**-100, 2.0**100
LINES = 32
EARLY = (0, 1, 3)
TAIL = 3 * LINES
SHARE = 0.1
QA, QB = 4 * ROWS, 4 * HALF
MESSAGE = 5 * ROWS + HALF


def move(value, target):
    pairs = []
    for x in range(NX):
        for zh in range(NZH):
            for y in range(NY):
                for zl in range(NZL):
                    for c in range(NC):
                        a, b, d, e, f = target(x, zh, y, zl, c)
                        src = (((x * NZH + zh) * NY + y) * NZL + zl) * NC + c
                        dst = (((a * NZH + b) * NY + d) * NZL + e) * NC + f
                        pairs.append((src, dst))
    return lax.ppermute(value, ("seq", "head"), pairs)


def params(mib):
    return pltpu.CompilerParams(vmem_limit_bytes=mib * 2**20)


def cost(flops, moved, exps=0):
    return pl.CostEstimate(flops=int(flops * SHARE), bytes_accessed=int(moved * SHARE), transcendentals=int(exps * SHARE))


def project_kernel(place, fine, coarse, wq, wk, wv, *refs):
    outs, more, rows, held, ready, sems = refs[:4], refs[4:5], refs[5], refs[6], refs[7], refs[8]
    steps = D // COLS
    pulls = [
        pltpu.make_async_copy(fine, rows.at[:FINE_ROWS], sems.at[0]),
        pltpu.make_async_copy(coarse, rows.at[FINE_ROWS:], sems.at[1]),
    ]
    for i, w in enumerate((wk, wv, wq)):
        for k in range(steps):
            span = slice(k * COLS, (k + 1) * COLS)
            pulls.append(pltpu.make_async_copy(w.at[span], held.at[i, span], sems.at[2 + i * steps + k]))
    for pull in pulls:
        pull.start()
    for pull in pulls[:2]:
        pull.wait()
    for i, base in enumerate((ROWS + HALF, 3 * ROWS + HALF, 0)):
        for k in range(steps):
            pulls[2 + i * steps + k].wait()
        for at in (0, HALF):
            total = None
            for k in range(0, D, COLS):
                part = jnp.dot(rows[at : at + HALF, k : k + COLS], held[i, k : k + COLS, :], preferred_element_type=F32)
                total = part if total is None else total + part
            total = total.astype(BF)
            for u in range(4):
                ready[u, base + at : base + at + HALF, :] = total[:, u * HD : (u + 1) * HD]
                shared = total[:, (4 + u // 2) * HD : (5 + u // 2) * HD]
                if base:
                    ready[u, base + ROWS + at : base + ROWS + at + HALF, :] = shared
                elif u % 2 == at // HALF:
                    ready[u, ROWS : ROWS + HALF, :] = shared
    for p in range(4):
        outs[p][...] = ready[lax.rem(place[0] + p, 4)]
    for i, p in enumerate(EARLY):
        more[0][4 * i * ROWS : 4 * (i + 1) * ROWS, :] = ready[lax.rem(place[0] + p, 4), ROWS + HALF :, :]


def project(place, fine, coarse, wq, wk, wv):
    smem, hbm = pl.BlockSpec(memory_space=pltpu.SMEM), pl.BlockSpec(memory_space=pl.ANY)
    return pl.pallas_call(
        project_kernel,
        in_specs=[smem] + [hbm] * 5,
        out_shape=[jax.ShapeDtypeStruct((MESSAGE, HD), BF)] * 4 + [jax.ShapeDtypeStruct((4 * ROWS * len(EARLY), HD), BF)],
        scratch_shapes=[
            pltpu.VMEM((ROWS, D), BF),
            pltpu.VMEM((3, D, COLS), BF),
            pltpu.VMEM((4, MESSAGE, HD), BF),
            pltpu.SemaphoreType.DMA((2 + 3 * D // COLS,)),
        ],
        compiler_params=params(60),
        cost_estimate=cost(6 * ROWS * D * COLS, 2 * D * (ROWS + 3 * COLS)),
        name="project",
    )(place, fine, coarse, wq, wk, wv)


def put(m, out, p, count):
    base = m.shape[0] - 4 * ROWS
    for i, quarter in enumerate((0, 2, 1, 3)):
        at = (count * i + p) * ROWS
        out[at : at + ROWS, :] = m[base + quarter * ROWS : base + (quarter + 1) * ROWS, :]


def stack_kernel(m0, m1, m2, m3, *refs):
    q, here, some = refs[-3:]
    for p, m in enumerate((m0, m1, m2, m3)):
        q[p * ROWS : (p + 1) * ROWS, :] = m[:ROWS, :]
        q[QA + p * HALF : QA + (p + 1) * HALF, :] = m[ROWS : ROWS + HALF, :]
        put(m, here, p, 4)
    some[...] = m2[ROWS + HALF :, :]


def halves_kernel(up, down, *refs):
    n = refs[-1].shape[0]
    refs[-2][...] = up[:n, :]
    refs[-1][...] = down[n:, :]


def join_kernel(m0, m1, m2, m3, out):
    for p, m in enumerate((m0, m1, m2, m3)):
        put(m, out, p, 4)


def arrange(kernel, inputs, after, sizes, name):
    vmem, anywhere = pl.BlockSpec(memory_space=pltpu.VMEM), pl.BlockSpec(memory_space=pl.ANY)
    return pl.pallas_call(
        kernel,
        in_specs=[vmem] * len(inputs) + [anywhere] * len(after),
        out_shape=[jax.ShapeDtypeStruct((n, HD), BF) for n in sizes],
        compiler_params=params(16),
        cost_estimate=cost(0, 4 * sum(sizes) * HD),
        name=name,
    )(*inputs, *after)


def fetch_kernel(blocks, w, *refs):
    held, sems = refs[-2:]
    pulls = []
    for n in range(4):
        cols = pl.ds(pl.multiple_of(blocks[n] * COLS, COLS), COLS)
        pulls.append(pltpu.make_async_copy(w.at[:, cols], held.at[n], sems.at[n]))
        pulls[n].start()
    for pull in pulls:
        pull.wait()


def fetch(blocks, w, after):
    anywhere = pl.BlockSpec(memory_space=pl.ANY)
    return pl.pallas_call(
        fetch_kernel,
        in_specs=[pl.BlockSpec(memory_space=pltpu.SMEM)] + [anywhere] * (1 + len(after)),
        out_specs=pl.BlockSpec(memory_space=pltpu.VMEM),
        out_shape=jax.ShapeDtypeStruct((4, COLS, COLS), BF),
        scratch_shapes=[pltpu.SemaphoreType.DMA((4,))],
        compiler_params=params(16),
        cost_estimate=cost(0, 16 * COLS * COLS),
        name="fetch",
    )(blocks, w, *after)


def dot_t(a, b):
    return lax.dot_general(a, b, (((1,), (1,)), ((), ())), preferred_element_type=F32)


def key_blocks(kvs):
    for kv in kvs:
        n = kv.shape[0] // 2
        for at in range(0, n, 512):
            end = min(at + 512, n)
            v = kv[n + at : n + end, :]
            yield kv[at:end, :], jnp.concatenate([v, jnp.ones_like(v)], axis=1)


def quick_block(q, kvs):
    both = None
    for k, v in key_blocks(kvs):
        part = jnp.dot(jnp.exp2(dot_t(q, k) * SCALE).astype(BF), v, preferred_element_type=F32)
        both = part if both is None else both + part
    total = both[:, HD:]
    return both[:, :HD] / total, jnp.log2(total), total


def careful_block(q, kvs):
    top = jnp.full((q.shape[0], 1), -jnp.inf, F32)
    both = jnp.zeros((q.shape[0], 2 * HD), F32)
    for k, v in key_blocks(kvs):
        s = dot_t(q, k) * SCALE
        new = jnp.maximum(top, jnp.max(s, axis=1, keepdims=True))
        both = both * jnp.exp2(top - new) + jnp.dot(jnp.exp2(s - new).astype(BF), v, preferred_element_type=F32)
        top = new
    return both[:, :HD] / both[:, HD:], top + jnp.log2(both[:, HD:])


def encode(out, logs):
    lines = []
    for start in range(0, QA + QB, HD):
        n = min(HD, QA + QB - start)
        same = lax.broadcasted_iota(jnp.int32, (n, HD), 0) == lax.broadcasted_iota(jnp.int32, (n, HD), 1)
        lines.append(jnp.sum(jnp.where(same, logs[start : start + n, :], 0.0), axis=0, keepdims=True))
    lines += [jnp.zeros((1, HD), F32)] * (LINES - len(lines))
    left = jnp.concatenate(lines, axis=0)
    for term in range(3):
        piece = left.astype(BF)
        out[QA + QB + LINES * term : QA + QB + LINES * (term + 1), :] = piece
        left = left - piece.astype(F32)


def attend_kernel(nq, *refs):
    qs, here, there, (out, logs, low, high) = refs[:nq], refs[nq], refs[nq + 1], refs[-4:]
    low[...] = jnp.full_like(low, 1.0)
    high[...] = jnp.full_like(high, 1.0)
    each = (QA + QB) // nq
    jobs = (
        (0, QA, [kv.at[: 2 * QA] for kv in (here, there)]),
        (QA, QA + QB, [kv.at[2 * QA :] for kv in (here, there)]),
    )
    for first, last, keys in jobs:
        for at in range(first, last, ROWS):
            rows, sums, total = quick_block(qs[at // each][at % each : at % each + ROWS, :], keys)
            out[at : at + ROWS, :] = rows.astype(BF)
            logs[at : at + ROWS, :] = sums
            eight = total.reshape(ROWS // 8, 8, HD)
            low[...] = jnp.minimum(low[...], jnp.min(eight, axis=0))
            high[...] = jnp.maximum(high[...], jnp.max(eight, axis=0))
    good = jnp.logical_and(jnp.min(low[...]) >= LOW, jnp.max(high[...]) <= HIGH)

    @pl.when(jnp.logical_not(good))
    def _():
        for n, q in enumerate(qs):
            for first, last, keys in jobs:
                start, end = max(first, n * each), min(last, (n + 1) * each)

                def again(step, _):
                    at = pl.multiple_of(start + step * HALF, HALF)
                    rows, sums = careful_block(q[pl.ds(at - n * each, HALF), :], keys)
                    out[pl.ds(at, HALF), :] = rows.astype(BF)
                    logs[pl.ds(at, HALF), :] = sums
                    return 0

                if start < end:
                    lax.fori_loop(0, (end - start) // HALF, again, 0)

    encode(out, logs)


def attend(qs, kvs, name, after=()):
    pairs = 2 * QA * (QA + QB)
    vmem, anywhere = pl.BlockSpec(memory_space=pltpu.VMEM), pl.BlockSpec(memory_space=pl.ANY)
    return pl.pallas_call(
        functools.partial(attend_kernel, len(qs)),
        in_specs=[vmem] * (len(qs) + 2) + [anywhere] * len(after),
        out_shape=jax.ShapeDtypeStruct((QA + QB + TAIL, HD), BF),
        scratch_shapes=[pltpu.VMEM((QA + QB, HD), F32), pltpu.VMEM((8, HD), F32), pltpu.VMEM((8, HD), F32)],
        compiler_params=params(16),
        cost_estimate=cost(8 * pairs * HD, 2 * (2 * (QA + QB) + 8 * QA) * HD, pairs),
        name=name,
    )(*qs, *kvs, *after)


def merge_kernel(a, b, c, d, m0, m1, m2, m3):
    parts, outs = (a, b, c, d), (m0, m1, m2, m3)
    for start in range(0, QA + QB, HD):
        step = min(HD, QA + QB - start)
        line = start // HD
        same = lax.broadcasted_iota(jnp.int32, (step, HD), 0) == lax.broadcasted_iota(jnp.int32, (step, HD), 1)
        logs = []
        for r in parts:
            terms = [r[QA + QB + LINES * t : QA + QB + LINES * (t + 1), :][line : line + 1, :] for t in range(3)]
            left = jnp.concatenate([jnp.where(same, t, jnp.zeros((), BF)) for t in terms], axis=1)
            logs.append(jnp.dot(left, jnp.ones((3 * HD, HD), BF), preferred_element_type=F32))
        top = functools.reduce(jnp.maximum, logs)
        shares = [jnp.exp2(l - top) for l in logs]
        mixed = sum(r[start : start + step, :].astype(F32) * s for r, s in zip(parts, shares))
        value = (mixed / sum(shares)).astype(BF)
        done = 0
        while done < step:
            at = start + done
            rows, base, offset = (ROWS, 0, 0) if at < QA else (HALF, QA, ROWS)
            out, row = divmod(at - base, rows)
            n = min(step - done, rows - row)
            outs[out][offset + row : offset + row + n, :] = value[done : done + n]
            done += n


def merge(parts):
    return pl.pallas_call(
        merge_kernel,
        out_shape=[jax.ShapeDtypeStruct((ROWS + HALF, HD), BF)] * 4,
        compiler_params=params(24),
        cost_estimate=cost(20 * (QA + QB) * HD, 10 * (QA + QB) * HD),
        name="merge",
    )(*parts)


def out_kernel(first, n, place, *refs):
    slots, w, outs, heads = refs[:4], refs[4], refs[5:-1], refs[-1]
    for p in range(4):
        u = lax.rem(place[0] + p, 4)
        heads[u] = slots[p][:ROWS, :]
        heads[4 + u // 2, pl.ds(pl.multiple_of(lax.rem(u, 2) * HALF, HALF), HALF), :] = slots[p][ROWS:, :]
    rows = jnp.concatenate([heads[h] for h in range(6)], axis=1)
    for i in range(n):
        part = jnp.dot(rows, w[first + i], preferred_element_type=F32)
        if i < n - 1:
            outs[0][:, i * COLS : (i + 1) * COLS] = part.astype(BF)
        else:
            outs[-1][...] = part


def out_project(place, first, n, slots, w, name):
    smem, vmem = pl.BlockSpec(memory_space=pltpu.SMEM), pl.BlockSpec(memory_space=pltpu.VMEM)
    shapes = [jax.ShapeDtypeStruct((ROWS, COLS), F32)]
    if n > 1:
        shapes = [jax.ShapeDtypeStruct((ROWS, (n - 1) * COLS), BF)] + shapes
    return pl.pallas_call(
        functools.partial(out_kernel, first, n),
        in_specs=[smem] + [vmem] * 5,
        out_shape=shapes,
        scratch_shapes=[pltpu.VMEM((6, ROWS, HD), BF)],
        compiler_params=params(16),
        cost_estimate=cost(2 * n * ROWS * COLS * COLS, 2 * (n * COLS * COLS + 3 * ROWS * COLS)),
        name=name,
    )(place, *slots, w)


def add_kernel(a, b, out):
    out[...] = (a[...] + b[:, :COLS].astype(F32)).astype(BF)


def final_kernel(a, b, c, fine, coarse):
    total = a[...] + b[:, COLS:].astype(F32) + c[...].astype(F32)
    fine[...] = total[:FINE_ROWS].astype(BF)
    coarse[...] = total[FINE_ROWS:].astype(BF)


def local(fine, coarse, w_query, w_key, w_value, w_out):
    seq, head = lax.axis_index("seq"), lax.axis_index("head")
    ints = lambda *v: jnp.stack(v).astype(jnp.int32)
    place = ints(seq // 8)
    zl, c = head // 2, head % 2

    along_x = lambda d: lambda x, zh, y, zl, c: ((x + d) % 4, zh, y, zl, c)
    along_y = lambda d: lambda x, zh, y, zl, c: (x, zh, (y + d) % 4, zl, c)
    across_zh = lambda x, zh, y, zl, c: (x, 1 - zh, y, zl, c)
    across_zl = lambda x, zh, y, zl, c: (x, zh, y, 1 - zl, c)
    across_c = lambda x, zh, y, zl, c: (x, zh, y, zl, 1 - c)
    hop = lambda value, along, d: move(value, along(d)) if d else value

    messages = project(place, fine, coarse, w_query, w_key, w_value)
    far, near = (1 - zl) * 2, zl * 2
    w_blocks = fetch(ints(far + 1 - c, near + 1 - c, far + c, near + c), w_out, [messages[0]])
    arrived = [hop(m, along_x, d) for d, m in enumerate(messages[:4])]
    early = move(messages[4], across_zh)
    q0, here, some = arrange(stack_kernel, arrived, [w_blocks], [QA + QB, 4 * QA, QA], "stack")
    there = {2: move(some, across_zh)}
    for i, p in enumerate(EARLY):
        there[p] = hop(early[QA * i : QA * (i + 1)], along_x, p)

    up, down = move(q0, along_y(1)), move(q0, along_y(-1))
    halves = arrange(halves_kernel, [up, down], [], [(QA + QB) // 2] * 2, "halves")
    queries = {0: [q0], 1: [up], 3: [down], 2: [move(half, along_y(d)) for half, d in zip(halves, (1, -1))]}
    (there,) = arrange(join_kernel, [there[p] for p in range(4)], [], [4 * QA], "join")
    parts, last = [], [halves[0]]
    for d in (1, 3, 2, 0):
        last = [attend(queries[d], (here, there), f"attend_{d}", last if d else last + parts[:1])]
        parts.append(hop(last[0], along_y, -d))
    slots = [hop(m, along_x, -d) for d, m in enumerate(merge(parts))]

    other, own = out_project(place, 0, 3, slots, w_blocks, "out_most")
    other = move(other, across_c)
    sent = pl.pallas_call(
        add_kernel, out_shape=jax.ShapeDtypeStruct((ROWS, COLS), BF), compiler_params=params(16), name="add_far"
    )(own, other)
    arrived = move(sent, across_zl)
    (own,) = out_project(place, 3, 1, slots, w_blocks, "out_last")
    return tuple(
        pl.pallas_call(
            final_kernel,
            out_shape=[
                jax.ShapeDtypeStruct((FINE_ROWS, COLS), BF),
                jax.ShapeDtypeStruct((ROWS - FINE_ROWS, COLS), BF),
            ],
            compiler_params=params(16),
            name="add_near",
        )(own, other, arrived)
    )


def solution(mesh):
    return jax.shard_map(
        local,
        mesh=mesh,
        in_specs=(
            P("seq", None),
            P("seq", None),
            P(None, "head"),
            P(None, "head"),
            P(None, "head"),
            P("head", None),
        ),
        out_specs=(P("seq", "head"), P("seq", "head")),
        check_vma=False,
    )
```

```python
import functools
import math

import jax
import jax.numpy as jnp
from jax import lax
from jax.experimental import pallas as pl
from jax.experimental.pallas import tpu as pltpu
from jax.sharding import PartitionSpec as P

BF, F32 = jnp.bfloat16, jnp.float32
D = 3072
HD = 128
FINE_ROWS, ROWS = 320, 352
HALF = ROWS // 2
COLS = 768
NX, NZH, NY, NZL, NC = 4, 2, 4, 2, 2
SCALE = math.log2(math.e) / math.sqrt(HD)
LOW, HIGH = 2.0**-100, 2.0**100
LINES = 32
EARLY = (0, 1, 3)
TAIL = 3 * LINES
SHARE = 0.1
QA, QB = 4 * ROWS, 4 * HALF
MESSAGE = 5 * ROWS + HALF


def move(value, target):
    pairs = []
    for x in range(NX):
        for zh in range(NZH):
            for y in range(NY):
                for zl in range(NZL):
                    for c in range(NC):
                        a, b, d, e, f = target(x, zh, y, zl, c)
                        src = (((x * NZH + zh) * NY + y) * NZL + zl) * NC + c
                        dst = (((a * NZH + b) * NY + d) * NZL + e) * NC + f
                        pairs.append((src, dst))
    return lax.ppermute(value, ("seq", "head"), pairs)


def params(mib):
    return pltpu.CompilerParams(vmem_limit_bytes=mib * 2**20)


def cost(flops, moved, exps=0):
    return pl.CostEstimate(flops=int(flops * SHARE), bytes_accessed=int(moved * SHARE), transcendentals=int(exps * SHARE))


def project_kernel(place, fine, coarse, wq, wk, wv, *refs):
    outs, more, rows, held, ready, sems = refs[:4], refs[4:5], refs[5], refs[6], refs[7], refs[8]
    steps = D // COLS
    pulls = [
        pltpu.make_async_copy(fine, rows.at[:FINE_ROWS], sems.at[0]),
        pltpu.make_async_copy(coarse, rows.at[FINE_ROWS:], sems.at[1]),
    ]
    for i, w in enumerate((wk, wv, wq)):
        for k in range(steps):
            span = slice(k * COLS, (k + 1) * COLS)
            pulls.append(pltpu.make_async_copy(w.at[span], held.at[i, span], sems.at[2 + i * steps + k]))
    for pull in pulls:
        pull.start()
    for pull in pulls[:2]:
        pull.wait()
    for i, base in enumerate((ROWS + HALF, 3 * ROWS + HALF, 0)):
        for k in range(steps):
            pulls[2 + i * steps + k].wait()
        for at in (0, HALF):
            total = None
            for k in range(0, D, COLS):
                part = jnp.dot(rows[at : at + HALF, k : k + COLS], held[i, k : k + COLS, :], preferred_element_type=F32)
                total = part if total is None else total + part
            total = total.astype(BF)
            for u in range(4):
                ready[u, base + at : base + at + HALF, :] = total[:, u * HD : (u + 1) * HD]
                shared = total[:, (4 + u // 2) * HD : (5 + u // 2) * HD]
                if base:
                    ready[u, base + ROWS + at : base + ROWS + at + HALF, :] = shared
                elif u % 2 == at // HALF:
                    ready[u, ROWS : ROWS + HALF, :] = shared
    for p in range(4):
        outs[p][...] = ready[lax.rem(place[0] + p, 4)]
    for i, p in enumerate(EARLY):
        more[0][4 * i * ROWS : 4 * (i + 1) * ROWS, :] = ready[lax.rem(place[0] + p, 4), ROWS + HALF :, :]


def project(place, fine, coarse, wq, wk, wv):
    smem, hbm = pl.BlockSpec(memory_space=pltpu.SMEM), pl.BlockSpec(memory_space=pl.ANY)
    return pl.pallas_call(
        project_kernel,
        in_specs=[smem] + [hbm] * 5,
        out_shape=[jax.ShapeDtypeStruct((MESSAGE, HD), BF)] * 4 + [jax.ShapeDtypeStruct((4 * ROWS * len(EARLY), HD), BF)],
        scratch_shapes=[
            pltpu.VMEM((ROWS, D), BF),
            pltpu.VMEM((3, D, COLS), BF),
            pltpu.VMEM((4, MESSAGE, HD), BF),
            pltpu.SemaphoreType.DMA((2 + 3 * D // COLS,)),
        ],
        compiler_params=params(60),
        cost_estimate=cost(6 * ROWS * D * COLS, 2 * D * (ROWS + 3 * COLS)),
        name="project",
    )(place, fine, coarse, wq, wk, wv)


def put(m, out, p, count):
    base = m.shape[0] - 4 * ROWS
    for i, quarter in enumerate((0, 2, 1, 3)):
        at = (count * i + p) * ROWS
        out[at : at + ROWS, :] = m[base + quarter * ROWS : base + (quarter + 1) * ROWS, :]


def stack_kernel(m0, m1, m2, m3, *refs):
    q, here, some = refs[-3:]
    for p, m in enumerate((m0, m1, m2, m3)):
        q[p * ROWS : (p + 1) * ROWS, :] = m[:ROWS, :]
        q[QA + p * HALF : QA + (p + 1) * HALF, :] = m[ROWS : ROWS + HALF, :]
        put(m, here, p, 4)
    some[...] = m2[ROWS + HALF :, :]


def halves_kernel(up, down, *refs):
    n = refs[-1].shape[0]
    refs[-2][...] = up[:n, :]
    refs[-1][...] = down[n:, :]


def join_kernel(m0, m1, m2, m3, out):
    for p, m in enumerate((m0, m1, m2, m3)):
        put(m, out, p, 4)


def arrange(kernel, inputs, after, sizes, name):
    vmem, anywhere = pl.BlockSpec(memory_space=pltpu.VMEM), pl.BlockSpec(memory_space=pl.ANY)
    return pl.pallas_call(
        kernel,
        in_specs=[vmem] * len(inputs) + [anywhere] * len(after),
        out_shape=[jax.ShapeDtypeStruct((n, HD), BF) for n in sizes],
        compiler_params=params(16),
        cost_estimate=cost(0, 4 * sum(sizes) * HD),
        name=name,
    )(*inputs, *after)


def fetch_kernel(blocks, w, *refs):
    held, sems = refs[-2:]
    pulls = []
    for n in range(4):
        cols = pl.ds(pl.multiple_of(blocks[n] * COLS, COLS), COLS)
        pulls.append(pltpu.make_async_copy(w.at[:, cols], held.at[n], sems.at[n]))
        pulls[n].start()
    for pull in pulls:
        pull.wait()


def fetch(blocks, w, after):
    anywhere = pl.BlockSpec(memory_space=pl.ANY)
    return pl.pallas_call(
        fetch_kernel,
        in_specs=[pl.BlockSpec(memory_space=pltpu.SMEM)] + [anywhere] * (1 + len(after)),
        out_specs=pl.BlockSpec(memory_space=pltpu.VMEM),
        out_shape=jax.ShapeDtypeStruct((4, COLS, COLS), BF),
        scratch_shapes=[pltpu.SemaphoreType.DMA((4,))],
        compiler_params=params(16),
        cost_estimate=cost(0, 16 * COLS * COLS),
        name="fetch",
    )(blocks, w, *after)


def dot_t(a, b):
    return lax.dot_general(a, b, (((1,), (1,)), ((), ())), preferred_element_type=F32)


def key_blocks(kvs):
    for kv in kvs:
        n = kv.shape[0] // 2
        for at in range(0, n, 512):
            end = min(at + 512, n)
            v = kv[n + at : n + end, :]
            yield kv[at:end, :], jnp.concatenate([v, jnp.ones_like(v)], axis=1)


def quick_block(q, kvs):
    both = None
    for k, v in key_blocks(kvs):
        part = jnp.dot(jnp.exp2(dot_t(q, k) * SCALE).astype(BF), v, preferred_element_type=F32)
        both = part if both is None else both + part
    total = both[:, HD:]
    return both[:, :HD] / total, jnp.log2(total), total


def careful_block(q, kvs):
    top = jnp.full((q.shape[0], 1), -jnp.inf, F32)
    both = jnp.zeros((q.shape[0], 2 * HD), F32)
    for k, v in key_blocks(kvs):
        s = dot_t(q, k) * SCALE
        new = jnp.maximum(top, jnp.max(s, axis=1, keepdims=True))
        both = both * jnp.exp2(top - new) + jnp.dot(jnp.exp2(s - new).astype(BF), v, preferred_element_type=F32)
        top = new
    return both[:, :HD] / both[:, HD:], top + jnp.log2(both[:, HD:])


def encode(out, logs):
    lines = []
    for start in range(0, QA + QB, HD):
        n = min(HD, QA + QB - start)
        same = lax.broadcasted_iota(jnp.int32, (n, HD), 0) == lax.broadcasted_iota(jnp.int32, (n, HD), 1)
        lines.append(jnp.sum(jnp.where(same, logs[start : start + n, :], 0.0), axis=0, keepdims=True))
    lines += [jnp.zeros((1, HD), F32)] * (LINES - len(lines))
    left = jnp.concatenate(lines, axis=0)
    for term in range(3):
        piece = left.astype(BF)
        out[QA + QB + LINES * term : QA + QB + LINES * (term + 1), :] = piece
        left = left - piece.astype(F32)


def attend_kernel(nq, *refs):
    qs, here, there, (out, logs, low, high) = refs[:nq], refs[nq], refs[nq + 1], refs[-4:]
    low[...] = jnp.full_like(low, 1.0)
    high[...] = jnp.full_like(high, 1.0)
    each = (QA + QB) // nq
    jobs = (
        (0, QA, [kv.at[: 2 * QA] for kv in (here, there)]),
        (QA, QA + QB, [kv.at[2 * QA :] for kv in (here, there)]),
    )
    for first, last, keys in jobs:
        for at in range(first, last, ROWS):
            rows, sums, total = quick_block(qs[at // each][at % each : at % each + ROWS, :], keys)
            out[at : at + ROWS, :] = rows.astype(BF)
            logs[at : at + ROWS, :] = sums
            eight = total.reshape(ROWS // 8, 8, HD)
            low[...] = jnp.minimum(low[...], jnp.min(eight, axis=0))
            high[...] = jnp.maximum(high[...], jnp.max(eight, axis=0))
    good = jnp.logical_and(jnp.min(low[...]) >= LOW, jnp.max(high[...]) <= HIGH)

    @pl.when(jnp.logical_not(good))
    def _():
        for n, q in enumerate(qs):
            for first, last, keys in jobs:
                start, end = max(first, n * each), min(last, (n + 1) * each)

                def again(step, _):
                    at = pl.multiple_of(start + step * HALF, HALF)
                    rows, sums = careful_block(q[pl.ds(at - n * each, HALF), :], keys)
                    out[pl.ds(at, HALF), :] = rows.astype(BF)
                    logs[pl.ds(at, HALF), :] = sums
                    return 0

                if start < end:
                    lax.fori_loop(0, (end - start) // HALF, again, 0)

    encode(out, logs)


def attend(qs, kvs, name, after=()):
    pairs = 2 * QA * (QA + QB)
    vmem, anywhere = pl.BlockSpec(memory_space=pltpu.VMEM), pl.BlockSpec(memory_space=pl.ANY)
    return pl.pallas_call(
        functools.partial(attend_kernel, len(qs)),
        in_specs=[vmem] * (len(qs) + 2) + [anywhere] * len(after),
        out_shape=jax.ShapeDtypeStruct((QA + QB + TAIL, HD), BF),
        scratch_shapes=[pltpu.VMEM((QA + QB, HD), F32), pltpu.VMEM((8, HD), F32), pltpu.VMEM((8, HD), F32)],
        compiler_params=params(16),
        cost_estimate=cost(8 * pairs * HD, 2 * (2 * (QA + QB) + 8 * QA) * HD, pairs),
        name=name,
    )(*qs, *kvs, *after)


def merge_kernel(a, b, c, d, m0, m1, m2, m3):
    parts, outs = (a, b, c, d), (m0, m1, m2, m3)
    for start in range(0, QA + QB, HD):
        step = min(HD, QA + QB - start)
        line = start // HD
        same = lax.broadcasted_iota(jnp.int32, (step, HD), 0) == lax.broadcasted_iota(jnp.int32, (step, HD), 1)
        left = []
        for r in parts:
            terms = [r[QA + QB + LINES * t : QA + QB + LINES * (t + 1), :][line : line + 1, :] for t in range(3)]
            left.append(jnp.concatenate([jnp.where(same, t, jnp.zeros((), BF)) for t in terms], axis=1))
        spread = jnp.dot(jnp.concatenate(left, axis=0), jnp.ones((3 * HD, HD), BF), preferred_element_type=F32)
        logs = [spread[n * step : (n + 1) * step, :] for n in range(4)]
        top = functools.reduce(jnp.maximum, logs)
        shares = [jnp.exp2(l - top) for l in logs]
        mixed = sum(r[start : start + step, :].astype(F32) * s for r, s in zip(parts, shares))
        value = (mixed / sum(shares)).astype(BF)
        done = 0
        while done < step:
            at = start + done
            rows, base, offset = (ROWS, 0, 0) if at < QA else (HALF, QA, ROWS)
            out, row = divmod(at - base, rows)
            n = min(step - done, rows - row)
            outs[out][offset + row : offset + row + n, :] = value[done : done + n]
            done += n


def merge(parts):
    return pl.pallas_call(
        merge_kernel,
        out_shape=[jax.ShapeDtypeStruct((ROWS + HALF, HD), BF)] * 4,
        compiler_params=params(24),
        cost_estimate=cost(20 * (QA + QB) * HD, 10 * (QA + QB) * HD),
        name="merge",
    )(*parts)


def out_kernel(first, n, place, *refs):
    slots, w, outs, heads = refs[:4], refs[4], refs[5:-1], refs[-1]
    for p in range(4):
        u = lax.rem(place[0] + p, 4)
        heads[u] = slots[p][:ROWS, :]
        heads[4 + u // 2, pl.ds(pl.multiple_of(lax.rem(u, 2) * HALF, HALF), HALF), :] = slots[p][ROWS:, :]
    rows = jnp.concatenate([heads[h] for h in range(6)], axis=1)
    for i in range(n):
        part = jnp.dot(rows, w[first + i], preferred_element_type=F32)
        if i < n - 1:
            outs[0][:, i * COLS : (i + 1) * COLS] = part.astype(BF)
        else:
            outs[-1][...] = part


def out_project(place, first, n, slots, w, name):
    smem, vmem = pl.BlockSpec(memory_space=pltpu.SMEM), pl.BlockSpec(memory_space=pltpu.VMEM)
    shapes = [jax.ShapeDtypeStruct((ROWS, COLS), F32)]
    if n > 1:
        shapes = [jax.ShapeDtypeStruct((ROWS, (n - 1) * COLS), BF)] + shapes
    return pl.pallas_call(
        functools.partial(out_kernel, first, n),
        in_specs=[smem] + [vmem] * 5,
        out_shape=shapes,
        scratch_shapes=[pltpu.VMEM((6, ROWS, HD), BF)],
        compiler_params=params(16),
        cost_estimate=cost(2 * n * ROWS * COLS * COLS, 2 * (n * COLS * COLS + 3 * ROWS * COLS)),
        name=name,
    )(place, *slots, w)


def add_kernel(a, b, out):
    out[...] = (a[...] + b[:, :COLS].astype(F32)).astype(BF)


def final_kernel(a, b, c, fine, coarse):
    total = a[...] + b[:, COLS:].astype(F32) + c[...].astype(F32)
    fine[...] = total[:FINE_ROWS].astype(BF)
    coarse[...] = total[FINE_ROWS:].astype(BF)


def local(fine, coarse, w_query, w_key, w_value, w_out):
    seq, head = lax.axis_index("seq"), lax.axis_index("head")
    ints = lambda *v: jnp.stack(v).astype(jnp.int32)
    place = ints(seq // 8)
    zl, c = head // 2, head % 2

    along_x = lambda d: lambda x, zh, y, zl, c: ((x + d) % 4, zh, y, zl, c)
    along_y = lambda d: lambda x, zh, y, zl, c: (x, zh, (y + d) % 4, zl, c)
    across_zh = lambda x, zh, y, zl, c: (x, 1 - zh, y, zl, c)
    across_zl = lambda x, zh, y, zl, c: (x, zh, y, 1 - zl, c)
    across_c = lambda x, zh, y, zl, c: (x, zh, y, zl, 1 - c)
    hop = lambda value, along, d: move(value, along(d)) if d else value

    messages = project(place, fine, coarse, w_query, w_key, w_value)
    far, near = (1 - zl) * 2, zl * 2
    w_blocks = fetch(ints(far + 1 - c, near + 1 - c, far + c, near + c), w_out, [messages[0]])
    arrived = [hop(m, along_x, d) for d, m in enumerate(messages[:4])]
    early = move(messages[4], across_zh)
    q0, here, some = arrange(stack_kernel, arrived, [w_blocks], [QA + QB, 4 * QA, QA], "stack")
    there = {2: move(some, across_zh)}
    for i, p in enumerate(EARLY):
        there[p] = hop(early[QA * i : QA * (i + 1)], along_x, p)

    up, down = move(q0, along_y(1)), move(q0, along_y(-1))
    halves = arrange(halves_kernel, [up, down], [], [(QA + QB) // 2] * 2, "halves")
    queries = {0: [q0], 1: [up], 3: [down], 2: [move(half, along_y(d)) for half, d in zip(halves, (1, -1))]}
    (there,) = arrange(join_kernel, [there[p] for p in range(4)], [], [4 * QA], "join")
    parts, last = [], [halves[0]]
    for d in (1, 3, 2, 0):
        last = [attend(queries[d], (here, there), f"attend_{d}", last if d else last + parts[:1])]
        parts.append(hop(last[0], along_y, -d))
    slots = [hop(m, along_x, -d) for d, m in enumerate(merge(parts))]

    other, own = out_project(place, 0, 3, slots, w_blocks, "out_most")
    other = move(other, across_c)
    sent = pl.pallas_call(
        add_kernel, out_shape=jax.ShapeDtypeStruct((ROWS, COLS), BF), compiler_params=params(16), name="add_far"
    )(own, other)
    arrived = move(sent, across_zl)
    (own,) = out_project(place, 3, 1, slots, w_blocks, "out_last")
    return tuple(
        pl.pallas_call(
            final_kernel,
            out_shape=[
                jax.ShapeDtypeStruct((FINE_ROWS, COLS), BF),
                jax.ShapeDtypeStruct((ROWS - FINE_ROWS, COLS), BF),
            ],
            compiler_params=params(16),
            name="add_near",
        )(own, other, arrived)
    )


def solution(mesh):
    return jax.shard_map(
        local,
        mesh=mesh,
        in_specs=(
            P("seq", None),
            P("seq", None),
            P(None, "head"),
            P(None, "head"),
            P(None, "head"),
            P("head", None),
        ),
        out_specs=(P("seq", "head"), P("seq", "head")),
        check_vma=False,
    )
```

```python
import functools
import math

import jax
import jax.numpy as jnp
from jax import lax
from jax.experimental import pallas as pl
from jax.experimental.pallas import tpu as pltpu
from jax.sharding import PartitionSpec as P

BF, F32 = jnp.bfloat16, jnp.float32
D = 3072
HD = 128
FINE_ROWS, ROWS = 320, 352
HALF = ROWS // 2
COLS = 768
NX, NZH, NY, NZL, NC = 4, 2, 4, 2, 2
SCALE = math.log2(math.e) / math.sqrt(HD)
LOW, HIGH = 2.0**-100, 2.0**100
LINES = 32
EARLY = (0, 1, 3)
TAIL = 3 * LINES
SHARE = 0.1
QA, QB = 4 * ROWS, 4 * HALF
MESSAGE = 5 * ROWS + HALF


def move(value, target):
    pairs = []
    for x in range(NX):
        for zh in range(NZH):
            for y in range(NY):
                for zl in range(NZL):
                    for c in range(NC):
                        a, b, d, e, f = target(x, zh, y, zl, c)
                        src = (((x * NZH + zh) * NY + y) * NZL + zl) * NC + c
                        dst = (((a * NZH + b) * NY + d) * NZL + e) * NC + f
                        pairs.append((src, dst))
    return lax.ppermute(value, ("seq", "head"), pairs)


def params(mib):
    return pltpu.CompilerParams(vmem_limit_bytes=mib * 2**20)


def cost(flops, moved, exps=0):
    return pl.CostEstimate(flops=int(flops * SHARE), bytes_accessed=int(moved * SHARE), transcendentals=int(exps * SHARE))


def project_kernel(place, fine, coarse, wq, wk, wv, *refs):
    outs, more, rows, held, ready, sems = refs[:4], refs[4:5], refs[5], refs[6], refs[7], refs[8]
    steps = D // COLS
    pulls = [
        pltpu.make_async_copy(fine, rows.at[:FINE_ROWS], sems.at[0]),
        pltpu.make_async_copy(coarse, rows.at[FINE_ROWS:], sems.at[1]),
    ]
    for i, w in enumerate((wk, wv, wq)):
        for k in range(steps):
            span = slice(k * COLS, (k + 1) * COLS)
            pulls.append(pltpu.make_async_copy(w.at[span], held.at[i, span], sems.at[2 + i * steps + k]))
    for pull in pulls:
        pull.start()
    for pull in pulls[:2]:
        pull.wait()
    for i, base in enumerate((ROWS + HALF, 3 * ROWS + HALF, 0)):
        for k in range(steps):
            pulls[2 + i * steps + k].wait()
        for at in (0, HALF):
            total = None
            for k in range(0, D, COLS):
                part = jnp.dot(rows[at : at + HALF, k : k + COLS], held[i, k : k + COLS, :], preferred_element_type=F32)
                total = part if total is None else total + part
            total = total.astype(BF)
            for u in range(4):
                ready[u, base + at : base + at + HALF, :] = total[:, u * HD : (u + 1) * HD]
                shared = total[:, (4 + u // 2) * HD : (5 + u // 2) * HD]
                if base:
                    ready[u, base + ROWS + at : base + ROWS + at + HALF, :] = shared
                elif u % 2 == at // HALF:
                    ready[u, ROWS : ROWS + HALF, :] = shared
    for p in range(4):
        outs[p][...] = ready[lax.rem(place[0] + p, 4)]
    for i, p in enumerate(EARLY):
        more[0][4 * i * ROWS : 4 * (i + 1) * ROWS, :] = ready[lax.rem(place[0] + p, 4), ROWS + HALF :, :]


def project(place, fine, coarse, wq, wk, wv):
    smem, hbm = pl.BlockSpec(memory_space=pltpu.SMEM), pl.BlockSpec(memory_space=pl.ANY)
    return pl.pallas_call(
        project_kernel,
        in_specs=[smem] + [hbm] * 5,
        out_shape=[jax.ShapeDtypeStruct((MESSAGE, HD), BF)] * 4 + [jax.ShapeDtypeStruct((4 * ROWS * len(EARLY), HD), BF)],
        scratch_shapes=[
            pltpu.VMEM((ROWS, D), BF),
            pltpu.VMEM((3, D, COLS), BF),
            pltpu.VMEM((4, MESSAGE, HD), BF),
            pltpu.SemaphoreType.DMA((2 + 3 * D // COLS,)),
        ],
        compiler_params=params(60),
        cost_estimate=cost(6 * ROWS * D * COLS, 2 * D * (ROWS + 3 * COLS)),
        name="project",
    )(place, fine, coarse, wq, wk, wv)


def put(m, out, p, count):
    base = m.shape[0] - 4 * ROWS
    for i, quarter in enumerate((0, 2, 1, 3)):
        at = (count * i + p) * ROWS
        out[at : at + ROWS, :] = m[base + quarter * ROWS : base + (quarter + 1) * ROWS, :]


def stack_kernel(m0, m1, m2, m3, *refs):
    q, here, some = refs[-3:]
    for p, m in enumerate((m0, m1, m2, m3)):
        q[p * ROWS : (p + 1) * ROWS, :] = m[:ROWS, :]
        q[QA + p * HALF : QA + (p + 1) * HALF, :] = m[ROWS : ROWS + HALF, :]
        put(m, here, p, 4)
    some[...] = m2[ROWS + HALF :, :]


def halves_kernel(up, down, *refs):
    n = refs[-1].shape[0]
    refs[-2][...] = up[:n, :]
    refs[-1][...] = down[n:, :]


def join_kernel(m0, m1, m2, m3, out):
    for p, m in enumerate((m0, m1, m2, m3)):
        put(m, out, p, 4)


def arrange(kernel, inputs, after, sizes, name):
    vmem, anywhere = pl.BlockSpec(memory_space=pltpu.VMEM), pl.BlockSpec(memory_space=pl.ANY)
    return pl.pallas_call(
        kernel,
        in_specs=[vmem] * len(inputs) + [anywhere] * len(after),
        out_shape=[jax.ShapeDtypeStruct((n, HD), BF) for n in sizes],
        compiler_params=params(16),
        cost_estimate=cost(0, 4 * sum(sizes) * HD),
        name=name,
    )(*inputs, *after)


def fetch_kernel(blocks, w, *refs):
    held, sems = refs[-2:]
    pulls = []
    for n in range(4):
        cols = pl.ds(pl.multiple_of(blocks[n] * COLS, COLS), COLS)
        pulls.append(pltpu.make_async_copy(w.at[:, cols], held.at[n], sems.at[n]))
        pulls[n].start()
    for pull in pulls:
        pull.wait()


def fetch(blocks, w, after):
    anywhere = pl.BlockSpec(memory_space=pl.ANY)
    return pl.pallas_call(
        fetch_kernel,
        in_specs=[pl.BlockSpec(memory_space=pltpu.SMEM)] + [anywhere] * (1 + len(after)),
        out_specs=pl.BlockSpec(memory_space=pltpu.VMEM),
        out_shape=jax.ShapeDtypeStruct((4, COLS, COLS), BF),
        scratch_shapes=[pltpu.SemaphoreType.DMA((4,))],
        compiler_params=params(16),
        cost_estimate=cost(0, 16 * COLS * COLS),
        name="fetch",
    )(blocks, w, *after)


def dot_t(a, b):
    return lax.dot_general(a, b, (((1,), (1,)), ((), ())), preferred_element_type=F32)


def key_blocks(kvs):
    for kv in kvs:
        n = kv.shape[0] // 2
        for at in range(0, n, 512):
            end = min(at + 512, n)
            v = kv[n + at : n + end, :]
            yield kv[at:end, :], jnp.concatenate([v, jnp.ones_like(v)], axis=1)


def quick_block(q, kvs):
    both = None
    for k, v in key_blocks(kvs):
        part = jnp.dot(jnp.exp2(dot_t(q, k) * SCALE).astype(BF), v, preferred_element_type=F32)
        both = part if both is None else both + part
    total = both[:, HD:]
    return both[:, :HD] / total, jnp.log2(total), total


def careful_block(q, kvs):
    top = jnp.full((q.shape[0], 1), -jnp.inf, F32)
    both = jnp.zeros((q.shape[0], 2 * HD), F32)
    for k, v in key_blocks(kvs):
        s = dot_t(q, k) * SCALE
        new = jnp.maximum(top, jnp.max(s, axis=1, keepdims=True))
        both = both * jnp.exp2(top - new) + jnp.dot(jnp.exp2(s - new).astype(BF), v, preferred_element_type=F32)
        top = new
    return both[:, :HD] / both[:, HD:], top + jnp.log2(both[:, HD:])


def encode(out, logs):
    lines = []
    for start in range(0, QA + QB, HD):
        n = min(HD, QA + QB - start)
        same = lax.broadcasted_iota(jnp.int32, (n, HD), 0) == lax.broadcasted_iota(jnp.int32, (n, HD), 1)
        lines.append(jnp.sum(jnp.where(same, logs[start : start + n, :], 0.0), axis=0, keepdims=True))
    lines += [jnp.zeros((1, HD), F32)] * (LINES - len(lines))
    left = jnp.concatenate(lines, axis=0)
    for term in range(3):
        piece = left.astype(BF)
        out[QA + QB + LINES * term : QA + QB + LINES * (term + 1), :] = piece
        left = left - piece.astype(F32)


def attend_kernel(nq, *refs):
    qs, here, there, (out, logs, low, high) = refs[:nq], refs[nq], refs[nq + 1], refs[-4:]
    low[...] = jnp.full_like(low, 1.0)
    high[...] = jnp.full_like(high, 1.0)
    each = (QA + QB) // nq
    jobs = (
        (0, QA, [kv.at[: 2 * QA] for kv in (here, there)]),
        (QA, QA + QB, [kv.at[2 * QA :] for kv in (here, there)]),
    )
    for first, last, keys in jobs:
        for at in range(first, last, ROWS):
            rows, sums, total = quick_block(qs[at // each][at % each : at % each + ROWS, :], keys)
            out[at : at + ROWS, :] = rows.astype(BF)
            logs[at : at + ROWS, :] = sums
            eight = total.reshape(ROWS // 8, 8, HD)
            low[...] = jnp.minimum(low[...], jnp.min(eight, axis=0))
            high[...] = jnp.maximum(high[...], jnp.max(eight, axis=0))
    good = jnp.logical_and(jnp.min(low[...]) >= LOW, jnp.max(high[...]) <= HIGH)

    @pl.when(jnp.logical_not(good))
    def _():
        for n, q in enumerate(qs):
            for first, last, keys in jobs:
                start, end = max(first, n * each), min(last, (n + 1) * each)

                def again(step, _):
                    at = pl.multiple_of(start + step * HALF, HALF)
                    rows, sums = careful_block(q[pl.ds(at - n * each, HALF), :], keys)
                    out[pl.ds(at, HALF), :] = rows.astype(BF)
                    logs[pl.ds(at, HALF), :] = sums
                    return 0

                if start < end:
                    lax.fori_loop(0, (end - start) // HALF, again, 0)

    encode(out, logs)


def attend(qs, kvs, name, after=()):
    pairs = 2 * QA * (QA + QB)
    vmem, anywhere = pl.BlockSpec(memory_space=pltpu.VMEM), pl.BlockSpec(memory_space=pl.ANY)
    return pl.pallas_call(
        functools.partial(attend_kernel, len(qs)),
        in_specs=[vmem] * (len(qs) + 2) + [anywhere] * len(after),
        out_shape=jax.ShapeDtypeStruct((QA + QB + TAIL, HD), BF),
        scratch_shapes=[pltpu.VMEM((QA + QB, HD), F32), pltpu.VMEM((8, HD), F32), pltpu.VMEM((8, HD), F32)],
        compiler_params=params(16),
        cost_estimate=cost(8 * pairs * HD, 2 * (2 * (QA + QB) + 8 * QA) * HD, pairs),
        name=name,
    )(*qs, *kvs, *after)


def merge_kernel(a, b, c, d, m0, m1, m2, m3):
    parts, outs = (a, b, c, d), (m0, m1, m2, m3)
    for start in range(0, QA + QB, HD):
        step = min(HD, QA + QB - start)
        line = start // HD
        same = lax.broadcasted_iota(jnp.int32, (step, HD), 0) == lax.broadcasted_iota(jnp.int32, (step, HD), 1)
        left = []
        for r in parts:
            terms = [r[QA + QB + LINES * t : QA + QB + LINES * (t + 1), :][line : line + 1, :] for t in range(3)]
            left.append(jnp.concatenate([jnp.where(same, t, jnp.zeros((), BF)) for t in terms], axis=1))
        spread = jnp.dot(jnp.concatenate(left, axis=0), jnp.ones((3 * HD, HD), BF), preferred_element_type=F32)
        logs = [spread[n * step : (n + 1) * step, :] for n in range(4)]
        top = functools.reduce(jnp.maximum, logs)
        shares = [jnp.exp2(l - top) for l in logs]
        mixed = sum(r[start : start + step, :].astype(F32) * s for r, s in zip(parts, shares))
        value = (mixed / sum(shares)).astype(BF)
        done = 0
        while done < step:
            at = start + done
            rows, base, offset = (ROWS, 0, 0) if at < QA else (HALF, QA, ROWS)
            out, row = divmod(at - base, rows)
            n = min(step - done, rows - row)
            outs[out][offset + row : offset + row + n, :] = value[done : done + n]
            done += n


def merge(parts):
    return pl.pallas_call(
        merge_kernel,
        out_shape=[jax.ShapeDtypeStruct((ROWS + HALF, HD), BF)] * 4,
        compiler_params=params(24),
        cost_estimate=cost(20 * (QA + QB) * HD, 10 * (QA + QB) * HD),
        name="merge",
    )(*parts)


def out_kernel(first, n, place, *refs):
    slots, w, outs, heads = refs[:4], refs[4], refs[5:-1], refs[-1]
    for p in range(4):
        u = lax.rem(place[0] + p, 4)
        heads[u] = slots[p][:ROWS, :]
        heads[4 + u // 2, pl.ds(pl.multiple_of(lax.rem(u, 2) * HALF, HALF), HALF), :] = slots[p][ROWS:, :]
    rows = jnp.concatenate([heads[h] for h in range(6)], axis=1)
    for i in range(n):
        part = jnp.dot(rows, w[first + i], preferred_element_type=F32)
        if i < n - 1:
            outs[0][:, i * COLS : (i + 1) * COLS] = part.astype(BF)
        else:
            outs[-1][...] = part


def out_project(place, first, n, slots, w, name):
    smem, vmem = pl.BlockSpec(memory_space=pltpu.SMEM), pl.BlockSpec(memory_space=pltpu.VMEM)
    shapes = [jax.ShapeDtypeStruct((ROWS, COLS), F32)]
    if n > 1:
        shapes = [jax.ShapeDtypeStruct((ROWS, (n - 1) * COLS), BF)] + shapes
    return pl.pallas_call(
        functools.partial(out_kernel, first, n),
        in_specs=[smem] + [vmem] * 5,
        out_shape=shapes,
        scratch_shapes=[pltpu.VMEM((6, ROWS, HD), BF)],
        compiler_params=params(16),
        cost_estimate=cost(2 * n * ROWS * COLS * COLS, 2 * (n * COLS * COLS + 3 * ROWS * COLS)),
        name=name,
    )(place, *slots, w)


def add_kernel(a, b, out):
    out[...] = (a[...] + b[:, :COLS].astype(F32)).astype(BF)


def final_kernel(a, b, c, fine, coarse):
    total = a[...] + b[:, COLS:].astype(F32) + c[...].astype(F32)
    fine[...] = total[:FINE_ROWS].astype(BF)
    coarse[...] = total[FINE_ROWS:].astype(BF)


def local(fine, coarse, w_query, w_key, w_value, w_out):
    seq, head = lax.axis_index("seq"), lax.axis_index("head")
    ints = lambda *v: jnp.stack(v).astype(jnp.int32)
    place = ints(seq // 8)
    zl, c = head // 2, head % 2

    along_x = lambda d: lambda x, zh, y, zl, c: ((x + d) % 4, zh, y, zl, c)
    along_y = lambda d: lambda x, zh, y, zl, c: (x, zh, (y + d) % 4, zl, c)
    across_zh = lambda x, zh, y, zl, c: (x, 1 - zh, y, zl, c)
    across_zl = lambda x, zh, y, zl, c: (x, zh, y, 1 - zl, c)
    across_c = lambda x, zh, y, zl, c: (x, zh, y, zl, 1 - c)
    hop = lambda value, along, d: move(value, along(d)) if d else value

    messages = project(place, fine, coarse, w_query, w_key, w_value)
    far, near = (1 - zl) * 2, zl * 2
    w_blocks = fetch(ints(far + 1 - c, near + 1 - c, far + c, near + c), w_out, [messages[0]])
    arrived = [hop(m, along_x, d) for d, m in enumerate(messages[:4])]
    early = move(messages[4], across_zh)
    q0, here, some = arrange(stack_kernel, arrived, [w_blocks], [QA + QB, 4 * QA, QA], "stack")
    there = {2: move(some, across_zh)}
    for i, p in enumerate(EARLY):
        there[p] = hop(early[QA * i : QA * (i + 1)], along_x, p)

    up, down = move(q0, along_y(1)), move(q0, along_y(-1))
    queries = {0: [q0], 1: [up], 3: [down]}
    (there,) = arrange(join_kernel, [there[p] for p in range(4)], [], [4 * QA], "join")
    parts, last = [], []
    for d in (1, 3, 2, 0):
        last = [attend(queries[d], (here, there), f"attend_{d}", last if d else last + parts[:1])]
        parts.append(hop(last[0], along_y, -d))
        if d == 1:
            halves = arrange(halves_kernel, [up, down], last, [(QA + QB) // 2] * 2, "halves")
            queries[2] = [move(half, along_y(e)) for half, e in zip(halves, (1, -1))]
            last = last + [halves[0]]
    slots = [hop(m, along_x, -d) for d, m in enumerate(merge(parts))]

    other, own = out_project(place, 0, 3, slots, w_blocks, "out_most")
    other = move(other, across_c)
    sent = pl.pallas_call(
        add_kernel, out_shape=jax.ShapeDtypeStruct((ROWS, COLS), BF), compiler_params=params(16), name="add_far"
    )(own, other)
    arrived = move(sent, across_zl)
    (own,) = out_project(place, 3, 1, slots, w_blocks, "out_last")
    return tuple(
        pl.pallas_call(
            final_kernel,
            out_shape=[
                jax.ShapeDtypeStruct((FINE_ROWS, COLS), BF),
                jax.ShapeDtypeStruct((ROWS - FINE_ROWS, COLS), BF),
            ],
            compiler_params=params(16),
            name="add_near",
        )(own, other, arrived)
    )


def solution(mesh):
    return jax.shard_map(
        local,
        mesh=mesh,
        in_specs=(
            P("seq", None),
            P("seq", None),
            P(None, "head"),
            P(None, "head"),
            P(None, "head"),
            P("head", None),
        ),
        out_specs=(P("seq", "head"), P("seq", "head")),
        check_vma=False,
    )
```
